128 devices in a mesh: chain: 128 (over z, y, x, core).
Axes of the slice: x: 4, y: 4, z: 4, core: 2. Of those that a mesh axis runs over, the one named last changes fastest.
Arguments:
- sections: float32 [128, 2, 4, 2, 128, 128], P('chain'), may hold values from -1.2 to 1.2
- probes: float32 [2, 2, 128, 16384], P(None, None, None, 'chain'), may hold values from -6 to 6
Outputs:
- prefixes: float32 [128, 2, 4, 2, 128, 128], P('chain')
- reflected: float32 [2, 2, 128, 16384], P(None, None, None, 'chain')
- transmitted: float32 [2, 2, 128, 16384], P(None, None, None, 'chain')
The draws below stay inside these ranges and needn't reach their ends.
All inputs are finite; a program needn't handle non-finite values.
Results may differ from the reference program's by a relative error of at most 0.0003.
Values sent between devices are 32-bit elements; how exact they have to be, the bound alone decides.
No kernel may reach another device: no remote copies, remote signals or barrier semaphores. Data moves between devices by JAX's collectives and lax.ppermute only.
A program may use at most 128 MiB of HBM per device.

```python
import math
import jax
import jax.numpy as jnp
from jax import lax

P_SIZE = 128
FREQ = 2
INV_STEPS = 9
SECTIONS = 128
PROBES = 16384


def draw_sections(key, part):
    subkeys = jax.random.split(key, 6)
    full_shape = (SECTIONS, FREQ, 4, 2, P_SIZE, P_SIZE)
    refl_scale = (0.04 / (2.0 * P_SIZE)) ** 0.5
    mix_scale = (0.05 / (2.0 * P_SIZE)) ** 0.5
    jitter = jax.random.truncated_normal(subkeys[0], -6.0, 6.0, full_shape, jnp.float32)
    scales = jnp.array([refl_scale, mix_scale, mix_scale, refl_scale], jnp.float32).reshape(1, 1, 4, 1, 1, 1)
    jitter = jitter * scales
    loss_rates = jax.random.uniform(subkeys[1], (SECTIONS, FREQ, P_SIZE), jnp.float32, 0.5, 3.0)
    radius = jnp.sqrt(0.91 - loss_rates / SECTIONS)
    phases = jax.random.uniform(subkeys[2], (SECTIONS, FREQ, P_SIZE), jnp.float32, -math.pi, math.pi)
    unit_matrix = jnp.eye(P_SIZE, dtype=jnp.float32)
    diag_real = (radius * jnp.cos(phases))[..., None] * unit_matrix
    diag_imag = (radius * jnp.sin(phases))[..., None] * unit_matrix
    direct = jnp.stack([diag_real, diag_imag], axis=2)
    vacant = jnp.zeros_like(direct)
    base_blocks = jnp.stack([vacant, direct, direct, vacant], axis=2)
    cavity_start = jax.random.randint(subkeys[3], (), 0, SECTIONS - 1).astype(jnp.int32)
    section_ids = jnp.arange(SECTIONS, dtype=jnp.int32)
    mirror_flag = jnp.logical_or(section_ids == cavity_start, section_ids == cavity_start + 1).astype(jnp.float32)
    left_phase = jax.random.uniform(subkeys[4], (SECTIONS, FREQ, P_SIZE), jnp.float32, -math.pi, math.pi)
    right_phase = jax.random.uniform(subkeys[5], (SECTIONS, FREQ, P_SIZE), jnp.float32, -math.pi, math.pi)
    pass_phase = 0.5 * (left_phase + right_phase + math.pi)
    mirror_refl = 0.85
    mirror_pass = (0.93 - mirror_refl * mirror_refl) ** 0.5

    def diagonal_block(amplitude, angle):
        block_real = (amplitude * jnp.cos(angle))[..., None] * unit_matrix
        block_imag = (amplitude * jnp.sin(angle))[..., None] * unit_matrix
        return jnp.stack([block_real, block_imag], axis=2)
    mirror_left = diagonal_block(mirror_refl, left_phase)
    mirror_right = diagonal_block(mirror_refl, right_phase)
    mirror_through = diagonal_block(mirror_pass, pass_phase)
    mirror_blocks = jnp.stack([mirror_left, mirror_through, mirror_through, mirror_right], axis=2)
    flag_full = mirror_flag.reshape(SECTIONS, 1, 1, 1, 1, 1)
    blocks = flag_full * mirror_blocks + (1.0 - flag_full) * base_blocks
    return blocks + jitter * (1.0 - 0.9 * flag_full)


def steps_of(rng, extent, cuts, smallest, largest):
    def one(dim, blocks):
        steps = jax.random.uniform(jax.random.fold_in(jax.random.fold_in(rng, 6), dim), (blocks,), jnp.float32, smallest / len(cuts), largest / len(cuts))
        return jnp.repeat(jnp.exp(steps), extent[dim] // blocks).reshape((-1,) + (1,) * (len(extent) - dim - 1))

    gain = one(*cuts[0])
    for cut in cuts[1:]:
        gain = gain * one(*cut)
    return gain


def gaussian(key, shape, width, limit, cuts=(), kind=jnp.bfloat16):
    result = width * jax.random.normal(key, shape, jnp.float32)
    if cuts:
        result = result * steps_of(key, shape, cuts, -0.22, 0.18)
    return jnp.clip(result, -limit, limit).astype(kind)


def setup_inputs(seed: int = 0) -> dict:
    key_list = jax.random.split(jax.random.key(seed), 3)
    sections = draw_sections(jax.random.fold_in(key_list[2], 71), 0)
    probes = gaussian(key_list[1], (FREQ, 2, P_SIZE, PROBES), 1.0, 6.0, ((3, 128),), jnp.float32)
    return dict(sections=sections, probes=probes)


precise = lax.Precision.HIGHEST


def complex_product(former, latter):
    former_re = former[..., 0, :, :]
    former_im = former[..., 1, :, :]
    latter_re = latter[..., 0, :, :]
    latter_im = latter[..., 1, :, :]
    real_part = jnp.einsum("...ij,...jk->...ik", former_re, latter_re, precision=precise) - jnp.einsum("...ij,...jk->...ik", former_im, latter_im, precision=precise)
    imag_part = jnp.einsum("...ij,...jk->...ik", former_re, latter_im, precision=precise) + jnp.einsum("...ij,...jk->...ik", former_im, latter_re, precision=precise)
    return jnp.stack([real_part, imag_part], axis=-3)


def unit_like(block):
    vacant = jnp.zeros_like(block[..., 0, :, :])
    diagonal_one = vacant + jnp.eye(block.shape[-1], dtype=block.dtype)
    return jnp.stack([diagonal_one, vacant], axis=-3)


def scattering_identity(matrix):
    unit_block = unit_like(matrix[:, 0])
    vacant = jnp.zeros_like(unit_block)
    return jnp.stack([vacant, unit_block, unit_block, vacant], axis=1)


def redheffer(first, second):
    first_left, first_back, first_fore, first_right = first[:, 0], first[:, 1], first[:, 2], first[:, 3]
    second_left, second_back, second_fore, second_right = second[:, 0], second[:, 1], second[:, 2], second[:, 3]
    unit_block = unit_like(first_left)
    bounce = complex_product(second_left, first_right)
    system = unit_block - bounce
    resolvent = unit_block
    for iteration in range(INV_STEPS):
        resolvent = complex_product(resolvent, 2.0 * unit_block - complex_product(system, resolvent))
    leading = complex_product(first_back, resolvent)
    new_left = first_left + complex_product(leading, complex_product(second_left, first_fore))
    new_back = complex_product(leading, second_back)
    trailing = second_fore + complex_product(complex_product(second_fore, first_right), complex_product(resolvent, second_left))
    new_fore = complex_product(trailing, first_fore)
    new_right = second_right + complex_product(trailing, complex_product(first_right, second_back))
    return jnp.stack([new_left, new_back, new_fore, new_right], axis=1)


def reference(sections, probes):
    def advance(running, section_block):
        combined = redheffer(running, section_block)
        return combined, combined

    initial = scattering_identity(sections[0])
    chain_total, prefixes = lax.scan(advance, initial, sections)
    reflected = complex_product(chain_total[:, 0], probes)
    transmitted = complex_product(chain_total[:, 2], probes)
    return prefixes, reflected, transmitted
```

```python
import functools

import jax
import jax.numpy as jnp
from jax import lax
from jax.experimental import pallas as pl
from jax.experimental.pallas import tpu as pltpu
from jax.sharding import PartitionSpec as P

F32 = jnp.float32
BF16 = jnp.bfloat16
N = 128


def split(x):
    high = x.astype(BF16)
    return high, (x - high.astype(F32)).astype(BF16)


def stack(*rows):
    return jnp.concatenate(rows, axis=0)


def square(x):
    turned = jnp.concatenate([-x[:, N:], x[:, :N]], axis=1)
    return jnp.concatenate([x, turned], axis=0)


def dot(a, b):
    return lax.dot(a, b, preferred_element_type=F32)


def times1(rows, matrix):
    return dot(rows.astype(BF16), square(matrix.astype(BF16)))


def times3(rows, matrix):
    rows_high, rows_low = rows if isinstance(rows, tuple) else split(rows)
    high, low = matrix if isinstance(matrix, tuple) else split(matrix)
    wide = square(high)
    return dot(rows_high, wide) + dot(rows_low, wide) + dot(rows_high, square(low))


def unit():
    shape = (N, 2 * N)
    row = lax.broadcasted_iota(jnp.int32, shape, 0)
    column = lax.broadcasted_iota(jnp.int32, shape, 1)
    return (row == column).astype(F32)


def series(bounce, one):
    total = one + bounce
    power = bounce.astype(BF16)
    power = dot(power, square(power)).astype(BF16)
    for step in range(7):
        if step < 6:
            both = dot(stack(total.astype(BF16), power), square(power))
            total = total + both[:N]
            power = both[N:].astype(BF16)
        else:
            total = total + dot(total.astype(BF16), square(power))
    return total


def star(first, second):
    a11, a12, a21, a22 = first
    b11, b12, b21, b22 = second
    one = unit()
    left = split(stack(b11, b21))
    by_right = times3(left, a22)
    bounce, tail = by_right[:N], by_right[N:]
    by_fore = times3(left, a21)
    total = series(bounce, one)
    bounce = split(bounce)
    residual = (one - total) + times3(bounce, total)
    total = total + times1(total, residual)
    lead = split(stack(a12, tail))
    rows = (stack(bounce[0], lead[0]), stack(bounce[1], lead[1]))
    solved = times3(rows, total)
    residual = (one - total) + solved[:N]
    solved = solved[N:] + times1(solved[N:], residual)
    solved = split(solved)
    near = times3(solved, by_fore[:N])
    far = times3(solved, b12)
    return (
        a11 + near[:N],
        far[:N],
        by_fore[N:] + near[N:],
        b22 + far[N:],
    )


def load(ref, *index):
    return jnp.concatenate([ref[index + (0,)], ref[index + (1,)]], axis=1)


def store(ref, index, value):
    ref[index + (0,)] = value[:, :N]
    ref[index + (1,)] = value[:, N:]


def bit(level):
    return (lax.axis_index("chain") >> level) & 1


def mirrored(position, flag):
    return position + flag * (3 - 2 * position)


def first_kernel(sections, received, total, prefix):
    core = bit(0)
    later = bit(0) ^ bit(1)
    own = [load(sections, 0, core, mirrored(p, core)) for p in range(4)]
    other = [load(received, mirrored(p, core)) for p in range(4)]
    result = star(own, other)
    for p in range(4):
        store(total, (mirrored(p, later),), result[p])
        store(prefix, (1, mirrored(p, core)), result[p])

    @pl.when(core == 0)
    def _():
        prefix[0] = sections[0, 0]

    @pl.when(core == 1)
    def _():
        prefix[0] = received[...]


def total_kernel(level, own, received, total):
    flag = bit(level) ^ bit(level + 1)
    result = star([load(own, p) for p in range(4)], [load(received, 3 - p) for p in range(4)])
    for p in range(4):
        store(total, (mirrored(p, flag),), result[p])


def last_kernel(level, own, received, whole):
    flag = bit(level)
    result = star([load(own, p) for p in range(4)], [load(received, 3 - p) for p in range(4)])
    upper = flag == 1
    store(whole, (0,), jnp.where(upper, result[3], result[0]))
    store(whole, (1,), jnp.where(upper, result[1], result[2]))


def prefix_kernel(level, before, prefix, extended):
    flag = bit(level)

    @pl.when(flag == 1)
    def _():
        first = [load(before, p) for p in range(4)]
        for k in range(2):
            result = star(first, [load(prefix, k, p) for p in range(4)])
            for p in range(4):
                store(extended, (k, p), result[p])

    @pl.when(flag == 0)
    def _():
        extended[...] = prefix[...]


def part_kernel(level, keep, before, prefix, extended):
    flag = bit(level)
    core = bit(0)
    which = core if keep else 1 - core

    @pl.when(flag == 1)
    def _():
        first = [load(before, p) for p in range(4)]
        result = star(first, [load(prefix, which, p) for p in range(4)])
        for p in range(4):
            store(extended, (p,), result[p])

    @pl.when(flag == 0)
    def _():
        extended[...] = prefix[which]


def final_kernel(kept, received, whole, other, probes, prefixes, reflected, transmitted):
    core = bit(0)
    prefixes[0, core] = kept[...]
    prefixes[0, 1 - core] = received[...]
    for source, frequency in ((whole, core), (other, 1 - core)):
        rows = stack(load(source, 0), load(source, 1))
        result = times3(rows, load(probes, frequency))
        store(reflected, (frequency,), result[:N])
        store(transmitted, (frequency,), result[N:])


STAR_FLOPS = 2 * 256 * 256 * 128 * 60


def call(kernel, outs, *operands, stars=1):
    in_vmem = pl.BlockSpec(memory_space=pltpu.VMEM)
    shapes = [jax.ShapeDtypeStruct(shape, F32) for shape in outs]
    return pl.pallas_call(
        kernel,
        out_shape=shapes,
        in_specs=[in_vmem] * len(operands),
        out_specs=[in_vmem] * len(outs),
        compiler_params=pltpu.CompilerParams(vmem_limit_bytes=40 << 20),
        cost_estimate=pl.CostEstimate(
            flops=int(STAR_FLOPS * stars), bytes_accessed=2 << 20, transcendentals=0
        ),
    )(*operands)


def exchange(value, mask):
    count = lax.axis_size("chain")
    return lax.ppermute(value, "chain", [(i, i ^ mask) for i in range(count)])


MASKS = (1, 2, 6, 8, 24, 32, 96)
ONE = (4, 2, N, N)
TWO = (2, 4, 2, N, N)


def local(sections, probes):
    core = lax.axis_index("chain") & 1
    sent = lax.dynamic_index_in_dim(sections[0], 1 - core, 0, keepdims=False)
    received = exchange(sent, 1)
    total, prefix = call(first_kernel, [ONE, TWO], sections, received)
    for level in range(1, 6):
        received = exchange(total, MASKS[level])
        (total,) = call(functools.partial(total_kernel, level), [ONE], total, received)
        (prefix,) = call(
            functools.partial(prefix_kernel, level), [TWO], received, prefix, stars=2
        )
    received = exchange(total, MASKS[6])
    (whole,) = call(functools.partial(last_kernel, 6), [(2, 2, N, N)], total, received)
    other = exchange(whole, 1)
    (leaving,) = call(functools.partial(part_kernel, 6, False), [ONE], received, prefix)
    arrived = exchange(leaving, 1)
    (kept,) = call(functools.partial(part_kernel, 6, True), [ONE], received, prefix)
    return tuple(
        call(
            final_kernel,
            [(1,) + TWO, probes.shape, probes.shape],
            kept,
            arrived,
            whole,
            other,
            probes,
        )
    )


def solution(mesh):
    placed = (P("chain", None, None, None, None, None), P(None, None, None, "chain"))
    return jax.shard_map(
        local,
        mesh=mesh,
        in_specs=placed,
        out_specs=(placed[0], placed[1], placed[1]),
        check_vma=False,
    )
```

```python
import functools

import jax
import jax.numpy as jnp
from jax import lax
from jax.experimental import pallas as pl
from jax.experimental.pallas import tpu as pltpu
from jax.sharding import PartitionSpec as P

F32 = jnp.float32
BF16 = jnp.bfloat16
N = 128
STEPS = 6


def split(x):
    high = x.astype(BF16)
    return high, (x - high.astype(F32)).astype(BF16)


def stack(*rows):
    return jnp.concatenate(rows, axis=0)


def square(x):
    turned = jnp.concatenate([-x[:, N:], x[:, :N]], axis=1)
    return jnp.concatenate([x, turned], axis=0)


def dot(a, b):
    return lax.dot(a, b, preferred_element_type=F32)


def times1(rows, matrix):
    return dot(rows.astype(BF16), square(matrix.astype(BF16)))


def times3(rows, matrix):
    rows_high, rows_low = rows if isinstance(rows, tuple) else split(rows)
    high, low = matrix if isinstance(matrix, tuple) else split(matrix)
    wide = square(high)
    return dot(rows_high, wide) + dot(rows_low, wide) + dot(rows_high, square(low))


def unit():
    shape = (N, 2 * N)
    row = lax.broadcasted_iota(jnp.int32, shape, 0)
    column = lax.broadcasted_iota(jnp.int32, shape, 1)
    return (row == column).astype(F32)


def halves(firsts, b11s):
    one = unit()
    each = range(len(firsts))
    lefts = [split(b11) for b11 in b11s]
    bounces = [times3(lefts[i], firsts[i][3]) for i in each]
    totals = [one + bounces[i] for i in each]
    powers = [bounces[i].astype(BF16) for i in each]
    powers = [dot(powers[i], square(powers[i])).astype(BF16) for i in each]
    for _ in range(STEPS - 1):
        both = [dot(stack(totals[i].astype(BF16), powers[i]), square(powers[i])) for i in each]
        totals = [totals[i] + both[i][:N] for i in each]
        powers = [both[i][N:].astype(BF16) for i in each]
    totals = [totals[i] + dot(totals[i].astype(BF16), square(powers[i])) for i in each]
    fores = [times3(lefts[i], firsts[i][2]) for i in each]
    bounces = [split(bounces[i]) for i in each]
    residuals = [(one - totals[i]) + times3(bounces[i], totals[i]) for i in each]
    totals = [totals[i] + times1(totals[i], residuals[i]) for i in each]
    leads = [split(stack(firsts[i][1], firsts[i][3])) for i in each]
    rows = [(stack(bounces[i][0], leads[i][0]), stack(bounces[i][1], leads[i][1])) for i in each]
    solved = [times3(rows[i], totals[i]) for i in each]
    residuals = [(one - totals[i]) + solved[i][:N] for i in each]
    solved = [solved[i][N:] + times1(solved[i][N:], residuals[i]) for i in each]
    nears = [times3(solved[i], fores[i]) for i in each]
    return [
        (solved[i][:N], solved[i][N:], firsts[i][2] + nears[i][N:], firsts[i][0] + nears[i][:N])
        for i in each
    ]


def half(first, b11):
    return halves([first], [b11])[0]


def other_half(u, w, v, b12, b21, b22):
    left = split(b21)
    y = times3(left, w)
    s21 = times3(left, v)
    far = times3(stack(u, y), b12)
    return far[:N], s21, b22 + far[N:]


def star(first, second):
    b11, b12, b21, b22 = second
    u, w, v, s11 = half(first, b11)
    return (s11,) + other_half(u, w, v, b12, b21, b22)


def load(ref, *index):
    return jnp.concatenate([ref[index + (0,)], ref[index + (1,)]], axis=1)


def store(ref, index, value):
    ref[index + (0,)] = value[:, :N]
    ref[index + (1,)] = value[:, N:]


def bit(level):
    return (lax.axis_index("chain") >> level) & 1


def mirrored(position, flag):
    return position + flag * (3 - 2 * position)


def store_total(result, flip, leading, rest):
    turned = flip == 1
    store(leading, (), jnp.where(turned, result[0], result[3]))
    store(rest, (0,), jnp.where(turned, result[3], result[0]))
    store(rest, (1 + flip,), result[1])
    store(rest, (2 - flip,), result[2])


def first_kernel(sections, received, leading, rest, prefix):
    core = bit(0)
    own = [load(sections, 0, core, mirrored(p, core)) for p in range(4)]
    other = [load(received, mirrored(p, core)) for p in range(4)]
    result = star(own, other)
    store_total(result, core ^ bit(1), leading, rest)
    for p in range(4):
        store(prefix, (1, mirrored(p, core)), result[p])

    @pl.when(core == 0)
    def _():
        prefix[0] = sections[0, 0]

    @pl.when(core == 1)
    def _():
        prefix[0] = received[...]


def half_kernel(level, leading, rest, received, prefix, middle):
    firsts = [[load(rest, p) for p in range(3)] + [load(leading)]]
    b11 = load(received)
    flag = bit(level)

    @pl.when(flag == 1)
    def _():
        mirror = [[load(prefix, k, 3 - p) for p in range(4)] for k in range(2)]
        for k, blocks in enumerate(halves(firsts + mirror, [b11] * 3)):
            for p in range(4):
                store(middle, (k, p), blocks[p])

    @pl.when(flag == 0)
    def _():
        for p, block in enumerate(half(firsts[0], b11)):
            store(middle, (0, p), block)


def second_half(middle, which, received):
    u, w, v, s11 = [load(middle, which, p) for p in range(4)]
    b22, b21, b12 = [load(received, p) for p in range(3)]
    return (s11,) + other_half(u, w, v, b12, b21, b22)


def total_kernel(level, middle, received, leading, rest):
    store_total(second_half(middle, 0, received), bit(level) ^ bit(level + 1), leading, rest)


def prefix_kernel(level, middle, received, prefix, extended):
    flag = bit(level)

    @pl.when(flag == 1)
    def _():
        for k in range(2):
            result = second_half(middle, k + 1, received)
            for p in range(4):
                store(extended, (k, 3 - p), result[p])

    @pl.when(flag == 0)
    def _():
        extended[...] = prefix[...]


def last_kernel(level, middle, received, prefix, whole, leaving, kept):
    flag = bit(level)
    core = bit(0)
    result = second_half(middle, 0, received)
    upper = flag == 1
    store(whole, (0,), jnp.where(upper, result[3], result[0]))
    store(whole, (1,), jnp.where(upper, result[1], result[2]))

    @pl.when(flag == 1)
    def _():
        for target, which in ((leaving, 1 - core), (kept, core)):
            result = second_half(middle, 1 + which, received)
            for p in range(4):
                store(target, (3 - p,), result[p])

    @pl.when(flag == 0)
    def _():
        leaving[...] = prefix[1 - core]
        kept[...] = prefix[core]


def final_kernel(kept, received, whole, other, probes, prefixes, reflected, transmitted):
    core = bit(0)
    prefixes[0, core] = kept[...]
    prefixes[0, 1 - core] = received[...]
    for source, frequency in ((whole, core), (other, 1 - core)):
        rows = stack(load(source, 0), load(source, 1))
        result = times3(rows, load(probes, frequency))
        store(reflected, (frequency,), result[:N])
        store(transmitted, (frequency,), result[N:])


STAR_FLOPS = 2 * 256 * 256 * 128 * 60


def call(kernel, outs, *operands, stars=1, unread=()):
    in_vmem = pl.BlockSpec(memory_space=pltpu.VMEM)
    anywhere = pl.BlockSpec(memory_space=pl.ANY)
    shapes = [jax.ShapeDtypeStruct(shape, F32) for shape in outs]
    return pl.pallas_call(
        kernel,
        out_shape=shapes,
        in_specs=[in_vmem] * len(operands) + [anywhere] * len(unread),
        out_specs=[in_vmem] * len(outs),
        compiler_params=pltpu.CompilerParams(vmem_limit_bytes=40 << 20),
        cost_estimate=pl.CostEstimate(
            flops=int(STAR_FLOPS * stars), bytes_accessed=2 << 20, transcendentals=0
        ),
    )(*operands, *unread)


def exchange(value, mask):
    count = lax.axis_size("chain")
    return lax.ppermute(value, "chain", [(i, i ^ mask) for i in range(count)])


HALF_STARS = 4
MASKS = (1, 2, 6, 8, 24, 32, 96)
BLOCK = (2, N, N)
REST = (3,) + BLOCK
ONE = (4,) + BLOCK
TWO = (2,) + ONE


def local(sections, probes):
    core = lax.axis_index("chain") & 1
    sent = lax.dynamic_index_in_dim(sections[0], 1 - core, 0, keepdims=False)
    received = exchange(sent, 1)
    leading, rest, prefix = call(first_kernel, [BLOCK, REST, TWO], sections, received, stars=1)
    for level in range(1, 7):
        got_leading = exchange(leading, MASKS[level])
        got_rest = exchange(rest, MASKS[level])
        (middle,) = call(
            functools.partial(half_kernel, level),
            [(3,) + ONE],
            leading,
            rest,
            got_leading,
            prefix,
            stars=HALF_STARS,
        )
        if level < 6:
            leading, rest = call(
                functools.partial(total_kernel, level), [BLOCK, REST], middle, got_rest
            )
            (prefix,) = call(
                functools.partial(prefix_kernel, level), [TWO], middle, got_rest, prefix
            )
    whole, leaving, kept = call(
        functools.partial(last_kernel, 6),
        [(2,) + BLOCK, ONE, ONE],
        middle,
        got_rest,
        prefix,
    )
    other = exchange(whole, 1)
    arrived = exchange(leaving, 1)
    return tuple(
        call(
            final_kernel,
            [(1,) + TWO, probes.shape, probes.shape],
            kept,
            arrived,
            whole,
            other,
            probes,
        )
    )


def solution(mesh):
    placed = (P("chain", None, None, None, None, None), P(None, None, None, "chain"))
    return jax.shard_map(
        local,
        mesh=mesh,
        in_specs=placed,
        out_specs=(placed[0], placed[1], placed[1]),
        check_vma=False,
    )
```

```python
import functools

import jax
import jax.numpy as jnp
from jax import lax
from jax.experimental import pallas as pl
from jax.experimental.pallas import tpu as pltpu
from jax.sharding import PartitionSpec as P

F32 = jnp.float32
BF16 = jnp.bfloat16
N = 128
STEPS = 6


def split(x):
    high = x.astype(BF16)
    return high, (x - high.astype(F32)).astype(BF16)


def stack(*rows):
    return jnp.concatenate(rows, axis=0)


def square(x):
    turned = jnp.concatenate([-x[:, N:], x[:, :N]], axis=1)
    return jnp.concatenate([x, turned], axis=0)


def dot(a, b):
    return lax.dot(a, b, preferred_element_type=F32)


def times1(rows, matrix):
    return dot(rows.astype(BF16), square(matrix.astype(BF16)))


def times3(rows, matrix):
    rows_high, rows_low = rows if isinstance(rows, tuple) else split(rows)
    high, low = matrix if isinstance(matrix, tuple) else split(matrix)
    wide = square(high)
    return dot(rows_high, wide) + dot(rows_low, wide) + dot(rows_high, square(low))


def unit():
    shape = (N, 2 * N)
    row = lax.broadcasted_iota(jnp.int32, shape, 0)
    column = lax.broadcasted_iota(jnp.int32, shape, 1)
    return (row == column).astype(F32)


def halves(firsts, b11s):
    one = unit()
    each = range(len(firsts))
    lefts = [split(b11) for b11 in b11s]
    bounces = [times3(lefts[i], firsts[i][3]) for i in each]
    totals = [one + bounces[i] for i in each]
    powers = [bounces[i].astype(BF16) for i in each]
    powers = [dot(powers[i], square(powers[i])).astype(BF16) for i in each]
    for _ in range(STEPS - 1):
        both = [dot(stack(totals[i].astype(BF16), powers[i]), square(powers[i])) for i in each]
        totals = [totals[i] + both[i][:N] for i in each]
        powers = [both[i][N:].astype(BF16) for i in each]
    totals = [totals[i] + dot(totals[i].astype(BF16), square(powers[i])) for i in each]
    fores = [times3(lefts[i], firsts[i][2]) for i in each]
    bounces = [split(bounces[i]) for i in each]
    residuals = [(one - totals[i]) + times3(bounces[i], totals[i]) for i in each]
    totals = [totals[i] + times1(totals[i], residuals[i]) for i in each]
    leads = [split(stack(firsts[i][1], firsts[i][3])) for i in each]
    rows = [(stack(bounces[i][0], leads[i][0]), stack(bounces[i][1], leads[i][1])) for i in each]
    solved = [times3(rows[i], totals[i]) for i in each]
    residuals = [(one - totals[i]) + solved[i][:N] for i in each]
    solved = [solved[i][N:] + times1(solved[i][N:], residuals[i]) for i in each]
    nears = [times3(solved[i], fores[i]) for i in each]
    return [
        (solved[i][:N], solved[i][N:], firsts[i][2] + nears[i][N:], firsts[i][0] + nears[i][:N])
        for i in each
    ]


def half(first, b11):
    return halves([first], [b11])[0]


def other_half(u, w, v, b12, b21, b22):
    left = split(b21)
    y = times3(left, w)
    s21 = times3(left, v)
    far = times3(stack(u, y), b12)
    return far[:N], s21, b22 + far[N:]


def star(first, second):
    b11, b12, b21, b22 = second
    u, w, v, s11 = half(first, b11)
    return (s11,) + other_half(u, w, v, b12, b21, b22)


def load(ref, *index):
    return jnp.concatenate([ref[index + (0,)], ref[index + (1,)]], axis=1)


def store(ref, index, value):
    ref[index + (0,)] = value[:, :N]
    ref[index + (1,)] = value[:, N:]


def bit(level):
    return (lax.axis_index("chain") >> level) & 1


def mirrored(position, flag):
    return position + flag * (3 - 2 * position)


def store_total(result, flip, leading, rest):
    turned = flip == 1
    store(leading, (), jnp.where(turned, result[0], result[3]))
    store(rest, (0,), jnp.where(turned, result[3], result[0]))
    store(rest, (1 + flip,), result[1])
    store(rest, (2 - flip,), result[2])


def first_kernel(section, received, leading, rest, prefix):
    core = bit(0)
    own = [load(section, mirrored(p, core)) for p in range(4)]
    other = [load(received, mirrored(p, core)) for p in range(4)]
    result = star(own, other)
    store_total(result, core ^ bit(1), leading, rest)
    for p in range(4):
        store(prefix, (1, mirrored(p, core)), result[p])

    @pl.when(core == 0)
    def _():
        prefix[0] = section[...]

    @pl.when(core == 1)
    def _():
        prefix[0] = received[...]


def half_kernel(level, leading, rest, received, prefix, middle):
    firsts = [[load(rest, p) for p in range(3)] + [load(leading)]]
    b11 = load(received)
    flag = bit(level)

    @pl.when(flag == 1)
    def _():
        mirror = [[load(prefix, k, 3 - p) for p in range(4)] for k in range(2)]
        for k, blocks in enumerate(halves(firsts + mirror, [b11] * 3)):
            for p in range(4):
                store(middle, (k, p), blocks[p])

    @pl.when(flag == 0)
    def _():
        for p, block in enumerate(half(firsts[0], b11)):
            store(middle, (0, p), block)


def second_half(middle, which, received):
    u, w, v, s11 = [load(middle, which, p) for p in range(4)]
    b22, b21, b12 = [load(received, p) for p in range(3)]
    return (s11,) + other_half(u, w, v, b12, b21, b22)


def total_kernel(level, middle, received, leading, rest):
    store_total(second_half(middle, 0, received), bit(level) ^ bit(level + 1), leading, rest)


def prefix_kernel(level, middle, received, prefix, extended):
    flag = bit(level)

    @pl.when(flag == 1)
    def _():
        for k in range(2):
            result = second_half(middle, k + 1, received)
            for p in range(4):
                store(extended, (k, 3 - p), result[p])

    @pl.when(flag == 0)
    def _():
        extended[...] = prefix[...]


def last_kernel(level, middle, received, prefix, whole, leaving, kept):
    flag = bit(level)
    core = bit(0)
    result = second_half(middle, 0, received)
    upper = flag == 1
    store(whole, (0,), jnp.where(upper, result[3], result[0]))
    store(whole, (1,), jnp.where(upper, result[1], result[2]))

    @pl.when(flag == 1)
    def _():
        for target, which in ((leaving, 1 - core), (kept, core)):
            result = second_half(middle, 1 + which, received)
            for p in range(4):
                store(target, (3 - p,), result[p])

    @pl.when(flag == 0)
    def _():
        leaving[...] = prefix[1 - core]
        kept[...] = prefix[core]


def final_kernel(kept, received, whole, other, probes, prefixes, reflected, transmitted):
    core = bit(0)
    prefixes[0, core] = kept[...]
    prefixes[0, 1 - core] = received[...]
    for source, frequency in ((whole, core), (other, 1 - core)):
        rows = stack(load(source, 0), load(source, 1))
        result = times3(rows, load(probes, frequency))
        store(reflected, (frequency,), result[:N])
        store(transmitted, (frequency,), result[N:])


STAR_FLOPS = 2 * 256 * 256 * 128 * 60


def call(kernel, outs, *operands, stars=1, unread=()):
    in_vmem = pl.BlockSpec(memory_space=pltpu.VMEM)
    anywhere = pl.BlockSpec(memory_space=pl.ANY)
    shapes = [jax.ShapeDtypeStruct(shape, F32) for shape in outs]
    return pl.pallas_call(
        kernel,
        out_shape=shapes,
        in_specs=[in_vmem] * len(operands) + [anywhere] * len(unread),
        out_specs=[in_vmem] * len(outs),
        compiler_params=pltpu.CompilerParams(vmem_limit_bytes=40 << 20),
        cost_estimate=pl.CostEstimate(
            flops=int(STAR_FLOPS * stars), bytes_accessed=2 << 20, transcendentals=0
        ),
    )(*operands, *unread)


def exchange(value, mask):
    count = lax.axis_size("chain")
    return lax.ppermute(value, "chain", [(i, i ^ mask) for i in range(count)])


HALF_STARS = 4
MASKS = (1, 2, 6, 8, 24, 32, 96)
BLOCK = (2, N, N)
REST = (3,) + BLOCK
ONE = (4,) + BLOCK
TWO = (2,) + ONE


def local(sections, probes):
    core = lax.axis_index("chain") & 1
    sent = lax.dynamic_index_in_dim(sections[0], 1 - core, 0, keepdims=False)
    section = lax.dynamic_index_in_dim(sections[0], core, 0, keepdims=False)
    received = exchange(sent, 1)
    leading, rest, prefix = call(first_kernel, [BLOCK, REST, TWO], section, received)
    for level in range(1, 7):
        got_leading = exchange(leading, MASKS[level])
        got_rest = exchange(rest, MASKS[level])
        (middle,) = call(
            functools.partial(half_kernel, level),
            [(3,) + ONE],
            leading,
            rest,
            got_leading,
            prefix,
            stars=HALF_STARS,
        )
        if level < 6:
            leading, rest = call(
                functools.partial(total_kernel, level), [BLOCK, REST], middle, got_rest
            )
            (prefix,) = call(
                functools.partial(prefix_kernel, level), [TWO], middle, got_rest, prefix
            )
    whole, leaving, kept = call(
        functools.partial(last_kernel, 6),
        [(2,) + BLOCK, ONE, ONE],
        middle,
        got_rest,
        prefix,
    )
    other = exchange(whole, 1)
    arrived = exchange(leaving, 1)
    return tuple(
        call(
            final_kernel,
            [(1,) + TWO, probes.shape, probes.shape],
            kept,
            arrived,
            whole,
            other,
            probes,
        )
    )


def solution(mesh):
    placed = (P("chain", None, None, None, None, None), P(None, None, None, "chain"))
    return jax.shard_map(
        local,
        mesh=mesh,
        in_specs=placed,
        out_specs=(placed[0], placed[1], placed[1]),
        check_vma=False,
    )
```

```python
import functools

import jax
import jax.numpy as jnp
from jax import lax
from jax.experimental import pallas as pl
from jax.experimental.pallas import tpu as pltpu
from jax.sharding import PartitionSpec as P

F32 = jnp.float32
BF16 = jnp.bfloat16
N = 128
STEPS = 6


def split(x):
    high = x.astype(BF16)
    return high, (x - high.astype(F32)).astype(BF16)


def stack(*rows):
    return jnp.concatenate(rows, axis=0)


def square(x):
    turned = jnp.concatenate([-x[:, N:], x[:, :N]], axis=1)
    return jnp.concatenate([x, turned], axis=0)


def dot(a, b):
    return lax.dot(a, b, preferred_element_type=F32)


def times1(rows, matrix):
    return dot(rows.astype(BF16), square(matrix.astype(BF16)))


def times3(rows, matrix):
    rows_high, rows_low = rows if isinstance(rows, tuple) else split(rows)
    high, low = matrix if isinstance(matrix, tuple) else split(matrix)
    wide = square(high)
    return dot(rows_high, wide) + dot(rows_low, wide) + dot(rows_high, square(low))


def unit():
    shape = (N, 2 * N)
    row = lax.broadcasted_iota(jnp.int32, shape, 0)
    column = lax.broadcasted_iota(jnp.int32, shape, 1)
    return (row == column).astype(F32)


def halves(firsts, b11s):
    one = unit()
    each = range(len(firsts))
    lefts = [split(b11) for b11 in b11s]
    bounces = [times3(lefts[i], firsts[i][3]) for i in each]
    totals = [one + bounces[i] for i in each]
    powers = [bounces[i].astype(BF16) for i in each]
    powers = [dot(powers[i], square(powers[i])).astype(BF16) for i in each]
    for _ in range(STEPS - 1):
        both = [dot(stack(totals[i].astype(BF16), powers[i]), square(powers[i])) for i in each]
        totals = [totals[i] + both[i][:N] for i in each]
        powers = [both[i][N:].astype(BF16) for i in each]
    totals = [totals[i] + dot(totals[i].astype(BF16), square(powers[i])) for i in each]
    fores = [times3(lefts[i], firsts[i][2]) for i in each]
    bounces = [split(bounces[i]) for i in each]
    residuals = [(one - totals[i]) + times3(bounces[i], totals[i]) for i in each]
    totals = [totals[i] + times1(totals[i], residuals[i]) for i in each]
    leads = [split(stack(firsts[i][1], firsts[i][3])) for i in each]
    rows = [(stack(bounces[i][0], leads[i][0]), stack(bounces[i][1], leads[i][1])) for i in each]
    solved = [times3(rows[i], totals[i]) for i in each]
    residuals = [(one - totals[i]) + solved[i][:N] for i in each]
    solved = [solved[i][N:] + times1(solved[i][N:], residuals[i]) for i in each]
    nears = [times3(solved[i], fores[i]) for i in each]
    return [
        (solved[i][:N], solved[i][N:], firsts[i][2] + nears[i][N:], firsts[i][0] + nears[i][:N])
        for i in each
    ]


def half(first, b11):
    return halves([first], [b11])[0]


def other_half(u, w, v, b12, b21, b22):
    left = split(b21)
    y = times3(left, w)
    s21 = times3(left, v)
    far = times3(stack(u, y), b12)
    return far[:N], s21, b22 + far[N:]


def star(first, second):
    b11, b12, b21, b22 = second
    u, w, v, s11 = half(first, b11)
    return (s11,) + other_half(u, w, v, b12, b21, b22)


def load(ref, *index):
    return jnp.concatenate([ref[index + (0,)], ref[index + (1,)]], axis=1)


def store(ref, index, value):
    ref[index + (0,)] = value[:, :N]
    ref[index + (1,)] = value[:, N:]


def bit(level):
    return (lax.axis_index("chain") >> level) & 1


def mirrored(position, flag):
    return position + flag * (3 - 2 * position)


def store_total(result, flip, leading, rest):
    turned = flip == 1
    store(leading, (), jnp.where(turned, result[0], result[3]))
    store(rest, (0,), jnp.where(turned, result[3], result[0]))
    store(rest, (1 + flip,), result[1])
    store(rest, (2 - flip,), result[2])


def first_kernel(section, received, leading, rest, prefix):
    core = bit(0)
    own = [load(section, mirrored(p, core)) for p in range(4)]
    other = [load(received, mirrored(p, core)) for p in range(4)]
    result = star(own, other)
    store_total(result, core ^ bit(1), leading, rest)
    for p in range(4):
        store(prefix, (1, mirrored(p, core)), result[p])

    @pl.when(core == 0)
    def _():
        prefix[0] = section[...]

    @pl.when(core == 1)
    def _():
        prefix[0] = received[...]


def half_kernel(level, leading, rest, received, prefix, middle):
    firsts = [[load(rest, p) for p in range(3)] + [load(leading)]]
    b11 = load(received)
    flag = bit(level)

    @pl.when(flag == 1)
    def _():
        mirror = [[load(prefix, k, 3 - p) for p in range(4)] for k in range(2)]
        for k, blocks in enumerate(halves(firsts + mirror, [b11] * 3)):
            for p in range(4):
                store(middle, (k, p), blocks[p])

    @pl.when(flag == 0)
    def _():
        for p, block in enumerate(half(firsts[0], b11)):
            store(middle, (0, p), block)


def second_half(middle, which, received):
    u, w, v, s11 = [load(middle, which, p) for p in range(4)]
    if len(received) == 1:
        b22, b21, b12 = [load(received[0], p) for p in range(3)]
    else:
        odd = bit(0) == 1
        b22, b21, b12 = [
            jnp.where(odd, load(received[1], p), load(received[0], p)) for p in range(3)
        ]
    return (s11,) + other_half(u, w, v, b12, b21, b22)


def total_kernel(level, middle, *refs):
    *received, leading, rest = refs
    store_total(second_half(middle, 0, received), bit(level) ^ bit(level + 1), leading, rest)


def prefix_kernel(level, middle, prefix, *refs):
    *received, extended = refs
    flag = bit(level)

    @pl.when(flag == 1)
    def _():
        for k in range(2):
            result = second_half(middle, k + 1, received)
            for p in range(4):
                store(extended, (k, 3 - p), result[p])

    @pl.when(flag == 0)
    def _():
        extended[...] = prefix[...]


def last_kernel(level, middle, received, prefix, whole, leaving, kept):
    flag = bit(level)
    core = bit(0)
    result = second_half(middle, 0, [received])
    upper = flag == 1
    store(whole, (0,), jnp.where(upper, result[3], result[0]))
    store(whole, (1,), jnp.where(upper, result[1], result[2]))

    @pl.when(flag == 1)
    def _():
        for target, which in ((leaving, 1 - core), (kept, core)):
            result = second_half(middle, 1 + which, [received])
            for p in range(4):
                store(target, (3 - p,), result[p])

    @pl.when(flag == 0)
    def _():
        leaving[...] = prefix[1 - core]
        kept[...] = prefix[core]


def final_kernel(kept, received, whole, other, probes, prefixes, reflected, transmitted):
    core = bit(0)
    prefixes[0, core] = kept[...]
    prefixes[0, 1 - core] = received[...]
    for source, frequency in ((whole, core), (other, 1 - core)):
        rows = stack(load(source, 0), load(source, 1))
        result = times3(rows, load(probes, frequency))
        store(reflected, (frequency,), result[:N])
        store(transmitted, (frequency,), result[N:])


STAR_FLOPS = 2 * 256 * 256 * 128 * 60


def call(kernel, outs, *operands, stars=1, unread=()):
    in_vmem = pl.BlockSpec(memory_space=pltpu.VMEM)
    anywhere = pl.BlockSpec(memory_space=pl.ANY)
    shapes = [jax.ShapeDtypeStruct(shape, F32) for shape in outs]
    return pl.pallas_call(
        kernel,
        out_shape=shapes,
        in_specs=[in_vmem] * len(operands) + [anywhere] * len(unread),
        out_specs=[in_vmem] * len(outs),
        compiler_params=pltpu.CompilerParams(vmem_limit_bytes=40 << 20),
        cost_estimate=pl.CostEstimate(
            flops=int(STAR_FLOPS * stars), bytes_accessed=2 << 20, transcendentals=0
        ),
    )(*operands, *unread)


def exchange(value, mask):
    count = lax.axis_size("chain")
    return lax.ppermute(value, "chain", [(i, i ^ mask) for i in range(count)])


HALF_STARS = 4
MASKS = (1, 2, 6, 8, 24, 32, 96)
BLOCK = (2, N, N)
REST = (3,) + BLOCK
ONE = (4,) + BLOCK
TWO = (2,) + ONE


def local(sections, probes):
    core = lax.axis_index("chain") & 1
    sent = lax.dynamic_index_in_dim(sections[0], 1 - core, 0, keepdims=False)
    section = lax.dynamic_index_in_dim(sections[0], core, 0, keepdims=False)
    received = exchange(sent, 1)
    leading, rest, prefix = call(first_kernel, [BLOCK, REST, TWO], section, received)
    for level in range(1, 7):
        got_leading = exchange(leading, MASKS[level])
        if level == 1:
            count = lax.axis_size("chain")
            odd = lax.ppermute(rest, "chain", [(i, i ^ 2) for i in range(1, count, 2)])
            later, _ = lax.optimization_barrier((rest, got_leading))
            even = lax.ppermute(later, "chain", [(i, i ^ 2) for i in range(0, count, 2)])
            got_rest = (even, odd)
        else:
            got_rest = (exchange(rest, MASKS[level]),)
        (middle,) = call(
            functools.partial(half_kernel, level),
            [(3,) + ONE],
            leading,
            rest,
            got_leading,
            prefix,
            stars=HALF_STARS,
        )
        if level < 6:
            leading, rest = call(
                functools.partial(total_kernel, level), [BLOCK, REST], middle, *got_rest
            )
            (prefix,) = call(
                functools.partial(prefix_kernel, level), [TWO], middle, prefix, *got_rest
            )
    whole, leaving, kept = call(
        functools.partial(last_kernel, 6),
        [(2,) + BLOCK, ONE, ONE],
        middle,
        *got_rest,
        prefix,
    )
    other = exchange(whole, 1)
    arrived = exchange(leaving, 1)
    return tuple(
        call(
            final_kernel,
            [(1,) + TWO, probes.shape, probes.shape],
            kept,
            arrived,
            whole,
            other,
            probes,
        )
    )


def solution(mesh):
    placed = (P("chain", None, None, None, None, None), P(None, None, None, "chain"))
    return jax.shard_map(
        local,
        mesh=mesh,
        in_specs=placed,
        out_specs=(placed[0], placed[1], placed[1]),
        check_vma=False,
    )
```

```python
import functools

import jax
import jax.numpy as jnp
from jax import lax
from jax.experimental import pallas as pl
from jax.experimental.pallas import tpu as pltpu
from jax.sharding import PartitionSpec as P

F32 = jnp.float32
BF16 = jnp.bfloat16
N = 128
STEPS = 6


def split(x):
    high = x.astype(BF16)
    return high, (x - high.astype(F32)).astype(BF16)


def stack(*rows):
    return jnp.concatenate(rows, axis=0)


def square(x):
    turned = jnp.concatenate([-x[:, N:], x[:, :N]], axis=1)
    return jnp.concatenate([x, turned], axis=0)


def dot(a, b):
    return lax.dot(a, b, preferred_element_type=F32)


def times1(rows, matrix):
    return dot(rows.astype(BF16), square(matrix.astype(BF16)))


def times3(rows, matrix):
    rows_high, rows_low = rows if isinstance(rows, tuple) else split(rows)
    high, low = matrix if isinstance(matrix, tuple) else split(matrix)
    wide = square(high)
    return dot(rows_high, wide) + dot(rows_low, wide) + dot(rows_high, square(low))


def unit():
    shape = (N, 2 * N)
    row = lax.broadcasted_iota(jnp.int32, shape, 0)
    column = lax.broadcasted_iota(jnp.int32, shape, 1)
    return (row == column).astype(F32)


def halves(firsts, b11s):
    one = unit()
    each = range(len(firsts))
    lefts = [split(b11) for b11 in b11s]
    bounces = [times3(lefts[i], firsts[i][3]) for i in each]
    totals = [one + bounces[i] for i in each]
    powers = [bounces[i].astype(BF16) for i in each]
    powers = [dot(powers[i], square(powers[i])).astype(BF16) for i in each]
    for _ in range(STEPS - 1):
        both = [dot(stack(totals[i].astype(BF16), powers[i]), square(powers[i])) for i in each]
        totals = [totals[i] + both[i][:N] for i in each]
        powers = [both[i][N:].astype(BF16) for i in each]
    totals = [totals[i] + dot(totals[i].astype(BF16), square(powers[i])) for i in each]
    fores = [times3(lefts[i], firsts[i][2]) for i in each]
    bounces = [split(bounces[i]) for i in each]
    residuals = [(one - totals[i]) + times3(bounces[i], totals[i]) for i in each]
    totals = [totals[i] + times1(totals[i], residuals[i]) for i in each]
    leads = [split(stack(firsts[i][1], firsts[i][3])) for i in each]
    rows = [(stack(bounces[i][0], leads[i][0]), stack(bounces[i][1], leads[i][1])) for i in each]
    solved = [times3(rows[i], totals[i]) for i in each]
    residuals = [(one - totals[i]) + solved[i][:N] for i in each]
    solved = [solved[i][N:] + times1(solved[i][N:], residuals[i]) for i in each]
    nears = [times3(solved[i], fores[i]) for i in each]
    return [
        (solved[i][:N], solved[i][N:], firsts[i][2] + nears[i][N:], firsts[i][0] + nears[i][:N])
        for i in each
    ]


def half(first, b11):
    return halves([first], [b11])[0]


def other_half(u, w, v, b12, b21, b22):
    left = split(b21)
    y = times3(left, w)
    s21 = times3(left, v)
    far = times3(stack(u, y), b12)
    return far[:N], s21, b22 + far[N:]


def star(first, second):
    b11, b12, b21, b22 = second
    u, w, v, s11 = half(first, b11)
    return (s11,) + other_half(u, w, v, b12, b21, b22)


def load(ref, *index):
    return jnp.concatenate([ref[index + (0,)], ref[index + (1,)]], axis=1)


def store(ref, index, value):
    ref[index + (0,)] = value[:, :N]
    ref[index + (1,)] = value[:, N:]


def bit(level):
    return (lax.axis_index("chain") >> level) & 1


def mirrored(position, flag):
    return position + flag * (3 - 2 * position)


def store_total(result, flip, leading, rest):
    turned = flip == 1
    store(leading, (), jnp.where(turned, result[0], result[3]))
    store(rest, (0,), jnp.where(turned, result[3], result[0]))
    store(rest, (1 + flip,), result[1])
    store(rest, (2 - flip,), result[2])


def first_kernel(section, received, leading, rest, prefix):
    core = bit(0)
    own = [load(section, mirrored(p, core)) for p in range(4)]
    other = [load(received, mirrored(p, core)) for p in range(4)]
    result = star(own, other)
    store_total(result, core ^ bit(1), leading, rest)
    for p in range(4):
        store(prefix, (1, mirrored(p, core)), result[p])

    @pl.when(core == 0)
    def _():
        prefix[0] = section[...]

    @pl.when(core == 1)
    def _():
        prefix[0] = received[...]


def half_kernel(level, leading, rest, received, prefix, middle):
    firsts = [[load(rest, p) for p in range(3)] + [load(leading)]]
    b11 = load(received)
    flag = bit(level)

    @pl.when(flag == 1)
    def _():
        mirror = [[load(prefix, k, 3 - p) for p in range(4)] for k in range(2)]
        for k, blocks in enumerate(halves(firsts + mirror, [b11] * 3)):
            for p in range(4):
                store(middle, (k, p), blocks[p])

    @pl.when(flag == 0)
    def _():
        for p, block in enumerate(half(firsts[0], b11)):
            store(middle, (0, p), block)


def second_half(middle, which, received):
    u, w, v, s11 = [load(middle, which, p) for p in range(4)]
    if len(received) == 1:
        b22, b21, b12 = [load(received[0], p) for p in range(3)]
    else:
        odd = bit(0) == 1
        b22, b21, b12 = [
            jnp.where(odd, load(received[1], p), load(received[0], p)) for p in range(3)
        ]
    return (s11,) + other_half(u, w, v, b12, b21, b22)


def total_kernel(level, middle, *refs):
    *received, leading, rest = refs
    store_total(second_half(middle, 0, received), bit(level) ^ bit(level + 1), leading, rest)


def prefix_kernel(level, middle, prefix, *refs):
    *received, extended = refs
    flag = bit(level)

    @pl.when(flag == 1)
    def _():
        for k in range(2):
            result = second_half(middle, k + 1, received)
            for p in range(4):
                store(extended, (k, 3 - p), result[p])

    @pl.when(flag == 0)
    def _():
        extended[...] = prefix[...]


def last_kernel(level, middle, received, prefix, leaving, kept):
    flag = bit(level)
    core = bit(0)
    result = second_half(middle, 0, [received])
    upper = flag == 1
    store(leaving, (4,), jnp.where(upper, result[3], result[0]))
    store(leaving, (5,), jnp.where(upper, result[1], result[2]))

    @pl.when(flag == 1)
    def _():
        for target, which in ((leaving, 1 - core), (kept, core)):
            result = second_half(middle, 1 + which, [received])
            for p in range(4):
                store(target, (3 - p,), result[p])

    @pl.when(flag == 0)
    def _():
        leaving[:4] = prefix[1 - core]
        kept[...] = prefix[core]


def apply(source, probes, frequency):
    return times3(stack(load(source, 4), load(source, 5)), load(probes, frequency))


def own_kernel(leaving, probes, fields):
    result = apply(leaving, probes, bit(0))
    store(fields, (0,), result[:N])
    store(fields, (1,), result[N:])


def final_kernel(kept, received, fields, probes, prefixes, reflected, transmitted):
    core = bit(0)
    result = apply(received, probes, 1 - core)
    prefixes[0, core] = kept[...]
    prefixes[0, 1 - core] = received[:4]
    reflected[core] = fields[0]
    transmitted[core] = fields[1]
    store(reflected, (1 - core,), result[:N])
    store(transmitted, (1 - core,), result[N:])


STAR_FLOPS = 2 * 256 * 256 * 128 * 60


def call(kernel, outs, *operands, stars=1, unread=()):
    in_vmem = pl.BlockSpec(memory_space=pltpu.VMEM)
    anywhere = pl.BlockSpec(memory_space=pl.ANY)
    shapes = [jax.ShapeDtypeStruct(shape, F32) for shape in outs]
    return pl.pallas_call(
        kernel,
        out_shape=shapes,
        in_specs=[in_vmem] * len(operands) + [anywhere] * len(unread),
        out_specs=[in_vmem] * len(outs),
        compiler_params=pltpu.CompilerParams(vmem_limit_bytes=40 << 20),
        cost_estimate=pl.CostEstimate(
            flops=int(STAR_FLOPS * stars), bytes_accessed=2 << 20, transcendentals=0
        ),
    )(*operands, *unread)


def exchange(value, mask):
    count = lax.axis_size("chain")
    return lax.ppermute(value, "chain", [(i, i ^ mask) for i in range(count)])


HALF_STARS = 4
MASKS = (1, 2, 6, 8, 24, 32, 96)
BLOCK = (2, N, N)
REST = (3,) + BLOCK
ONE = (4,) + BLOCK
TWO = (2,) + ONE


def local(sections, probes):
    core = lax.axis_index("chain") & 1
    sent = lax.dynamic_index_in_dim(sections[0], 1 - core, 0, keepdims=False)
    section = lax.dynamic_index_in_dim(sections[0], core, 0, keepdims=False)
    received = exchange(sent, 1)
    leading, rest, prefix = call(first_kernel, [BLOCK, REST, TWO], section, received)
    for level in range(1, 7):
        got_leading = exchange(leading, MASKS[level])
        if level == 1:
            count = lax.axis_size("chain")
            odd = lax.ppermute(rest, "chain", [(i, i ^ 2) for i in range(1, count, 2)])
            later, _ = lax.optimization_barrier((rest, got_leading))
            even = lax.ppermute(later, "chain", [(i, i ^ 2) for i in range(0, count, 2)])
            got_rest = (even, odd)
        else:
            got_rest = (exchange(rest, MASKS[level]),)
        (middle,) = call(
            functools.partial(half_kernel, level),
            [(3,) + ONE],
            leading,
            rest,
            got_leading,
            prefix,
            stars=HALF_STARS,
        )
        if level < 6:
            leading, rest = call(
                functools.partial(total_kernel, level), [BLOCK, REST], middle, *got_rest
            )
            (prefix,) = call(
                functools.partial(prefix_kernel, level), [TWO], middle, prefix, *got_rest
            )
    leaving, kept = call(
        functools.partial(last_kernel, 6),
        [(6,) + BLOCK, ONE],
        middle,
        *got_rest,
        prefix,
    )
    arrived = exchange(leaving, 1)
    (fields,) = call(own_kernel, [(2,) + BLOCK], leaving, probes)
    return tuple(
        call(
            final_kernel,
            [(1,) + TWO, probes.shape, probes.shape],
            kept,
            arrived,
            fields,
            probes,
        )
    )


def solution(mesh):
    placed = (P("chain", None, None, None, None, None), P(None, None, None, "chain"))
    return jax.shard_map(
        local,
        mesh=mesh,
        in_specs=placed,
        out_specs=(placed[0], placed[1], placed[1]),
        check_vma=False,
    )
```
